32 devices in a mesh: member: 4 (over y, x), space: 8 (over z, core).
Axes of the slice: x: 2, y: 2, z: 4, core: 2. Of those that a mesh axis runs over, the one named last changes fastest.
Arguments:
- zonal_wind: bfloat16 [24, 64, 256, 128], P('member', 'space'), may hold values from -6 to 6
- meridional_wind: bfloat16 [24, 64, 256, 128], P('member', 'space'), may hold values from -6 to 6
- heat_anomaly: bfloat16 [24, 64, 256, 128], P('member', 'space'), may hold values from -6 to 6
- moisture_anomaly: bfloat16 [24, 64, 256, 128], P('member', 'space'), may hold values from -6 to 6
- projection_scale: float32 [64, 256], P('space'), may hold values from 0.5 to 2
- balance_multiplier: float32 [64, 256], P('space'), may hold values from -4 to 4
- heat_on_curl_slope: float32 [128], replicated, may hold values from 0.3 to 1.5
- moisture_on_heat_slope: float32 [128], replicated, may hold values from 0.3 to 1.5
Outputs:
- covariance: float32 [8, 512, 512], P('space', 'member')
The draws below stay inside these ranges and needn't reach their ends.
All inputs are finite; a program needn't handle non-finite values.
Results may differ from the reference program's by a relative error of at most 0.0009.
Values may be sent and summed in bfloat16 or wider, within the bound.
A program may use at most 128 MiB of HBM per device.

```python
import math
import jax
import jax.numpy as jnp
from jax import lax

HEIGHT_STEPS = 128
STATE = 512
STRIP_PARALLELS = 8
PATCH_MERIDIANS = 256
SAMPLE_COUNT = 24
BANDS = 8
GLOBE_PARALLELS = 64


def shard_levels(own_key, extent, shards, low, high):
    level, own = 1.0, jax.random.fold_in(own_key, 6)
    for position, shards_of in shards:
        heights = jnp.exp(jax.random.uniform(jax.random.fold_in(own, position), (shards_of,), jnp.float32, low / len(shards), high / len(shards)))
        level = level * jnp.repeat(heights, extent[position] // shards_of).reshape([-1 if axis == position else 1 for axis in range(len(extent))])
    return level


def gaussian(key, dims, spread, bound, pieces=(), held_as=jnp.bfloat16):
    result = jax.random.normal(key, dims, jnp.float32) * spread
    if len(pieces) > 0:
        result = shard_levels(key, dims, pieces, -0.22, 0.18) * result
    return jnp.clip(result, min=-bound, max=bound).astype(held_as)


def setup_inputs(seed: int = 0) -> dict:
    key_of = jax.random.split(jax.random.key(seed), 9)
    zonal_wind = gaussian(key_of[0], (SAMPLE_COUNT, GLOBE_PARALLELS, PATCH_MERIDIANS, HEIGHT_STEPS), 1.0, 6.0, ((0, 4), (1, 8)))
    meridional_wind = gaussian(key_of[1], (SAMPLE_COUNT, GLOBE_PARALLELS, PATCH_MERIDIANS, HEIGHT_STEPS), 1.0, 6.0, ((0, 4), (1, 8)))
    heat_anomaly = gaussian(key_of[2], (SAMPLE_COUNT, GLOBE_PARALLELS, PATCH_MERIDIANS, HEIGHT_STEPS), 1.0, 6.0, ((0, 4), (1, 8)))
    moisture_anomaly = gaussian(key_of[3], (SAMPLE_COUNT, GLOBE_PARALLELS, PATCH_MERIDIANS, HEIGHT_STEPS), 1.0, 6.0, ((0, 4), (1, 8)))
    projection_scale = jnp.clip(jnp.exp(math.log(2.0) - 1.3862944 * jax.random.uniform(key_of[4], (GLOBE_PARALLELS, PATCH_MERIDIANS), jnp.float32) ** shard_levels(key_of[4], (GLOBE_PARALLELS, PATCH_MERIDIANS), ((0, 8),), -0.2, 0.2)), 0.5, 2.0)
    balance_multiplier = gaussian(key_of[5], (GLOBE_PARALLELS, PATCH_MERIDIANS), 1.0, 4.0, ((0, 8),), jnp.float32)
    heat_on_curl_slope = jnp.clip(jax.random.uniform(key_of[6], (HEIGHT_STEPS,), jnp.float32, 0.3, 1.5), 0.3, 1.5)
    moisture_on_heat_slope = jnp.clip(jax.random.uniform(key_of[7], (HEIGHT_STEPS,), jnp.float32, 0.3, 1.5), 0.3, 1.5)
    return dict(zonal_wind=zonal_wind, meridional_wind=meridional_wind, heat_anomaly=heat_anomaly, moisture_anomaly=moisture_anomaly, projection_scale=projection_scale, balance_multiplier=balance_multiplier, heat_on_curl_slope=heat_on_curl_slope, moisture_on_heat_slope=moisture_on_heat_slope)


def lat_diff(padded):
    return (-padded[:, 4:] + 8.0 * padded[:, 3:-1] - 8.0 * padded[:, 1:-3] + padded[:, :-4]) / 12.0


def lon_diff(field):
    return (jnp.roll(field, -1, 2) - jnp.roll(field, 1, 2)) / 2.0


def derive_quantities(zonal_wind_bordered, meridional_wind_bordered, heat_anomaly, moisture_anomaly, projection_scale, balance_multiplier, heat_on_curl_slope, moisture_on_heat_slope):
    u_full = zonal_wind_bordered.astype(jnp.float32)
    v_full = meridional_wind_bordered.astype(jnp.float32)
    u_mid = u_full[:, 2:-2]
    v_mid = v_full[:, 2:-2]
    factor = projection_scale[None, :, :, None]
    wind_curl = factor * (lon_diff(v_mid) - lat_diff(u_full))
    wind_spreading = factor * (lon_diff(u_mid) + lat_diff(v_full))
    heat_residual = heat_anomaly.astype(jnp.float32) - heat_on_curl_slope * balance_multiplier[None, :, :, None] * wind_curl
    moisture_residual = moisture_anomaly.astype(jnp.float32) - moisture_on_heat_slope * heat_residual
    return jnp.concatenate([wind_curl, wind_spreading, heat_residual, moisture_residual], axis=3).astype(jnp.bfloat16)


def reference(zonal_wind, meridional_wind, heat_anomaly, moisture_anomaly, projection_scale, balance_multiplier, heat_on_curl_slope, moisture_on_heat_slope):
    u_pad = jnp.pad(zonal_wind, ((0, 0), (2, 2), (0, 0), (0, 0)))
    v_pad = jnp.pad(meridional_wind, ((0, 0), (2, 2), (0, 0), (0, 0)))

    def one_band(band):
        starting_parallel = (band * STRIP_PARALLELS).astype(jnp.int32)
        strip_zonal_wind = lax.dynamic_slice_in_dim(u_pad, starting_parallel, STRIP_PARALLELS + 4, 1)
        strip_meridional_wind = lax.dynamic_slice_in_dim(v_pad, starting_parallel, STRIP_PARALLELS + 4, 1)
        strip_heat = lax.dynamic_slice_in_dim(heat_anomaly, starting_parallel, STRIP_PARALLELS, 1)
        strip_moisture = lax.dynamic_slice_in_dim(moisture_anomaly, starting_parallel, STRIP_PARALLELS, 1)
        strip_scale_factor = lax.dynamic_slice_in_dim(projection_scale, starting_parallel, STRIP_PARALLELS, 0)
        strip_balance_factor = lax.dynamic_slice_in_dim(balance_multiplier, starting_parallel, STRIP_PARALLELS, 0)
        sample_vector = derive_quantities(strip_zonal_wind, strip_meridional_wind, strip_heat, strip_moisture, strip_scale_factor, strip_balance_factor, heat_on_curl_slope, moisture_on_heat_slope).astype(jnp.float32)
        ens_mean = jnp.sum(sample_vector, axis=0) / SAMPLE_COUNT
        anomaly = (sample_vector - ens_mean[None]).reshape(-1, STATE)
        moments = jnp.dot(anomaly.T, anomaly, preferred_element_type=jnp.float32, precision=lax.Precision.HIGHEST)
        return moments / ((SAMPLE_COUNT - 1) * STRIP_PARALLELS * PATCH_MERIDIANS)

    return lax.map(one_band, jnp.arange(BANDS, dtype=jnp.int32))
```

```python
import functools

import jax
import jax.numpy as jnp
from jax import lax
from jax.experimental import pallas as pl
from jax.experimental.pallas import tpu as pltpu
from jax.sharding import PartitionSpec as P

CHUNK = 16


def moments_kernel(rows, halo, *refs):
    u_hbm, v_hbm, h_hbm, q_hbm, f_hbm, c_hbm = refs[:6]
    refs = refs[6:]
    if halo:
        low_hbm, high_hbm, start_ref = refs[:3]
        refs = refs[3:]
    shift_ref, slope_ref, mean_ref, moment_ref = refs[:4]
    u, v, h, q, f, c, dlon, anom, wind_sem, rest_sem, halo_sem = refs[4:]
    members, extended, lons, levels = u.shape
    height = extended - 4
    need = sorted({r + d for r in rows for d in range(-2, 3)})
    own = [r for r in need if 0 <= r < height]
    wind_copies, rest_copies, halo_copies = {}, {}, []
    for r in own:
        wind_copies[r] = [
            pltpu.make_async_copy(src.at[:, r], dst.at[:, r + 2], wind_sem.at[r, k])
            for k, (src, dst) in enumerate(((u_hbm, u), (v_hbm, v)))
        ]
    for k, r in enumerate(rows):
        rest_copies[k] = [
            pltpu.make_async_copy(h_hbm.at[:, r], h.at[k], rest_sem.at[k, 0]),
            pltpu.make_async_copy(q_hbm.at[:, r], q.at[k], rest_sem.at[k, 1]),
            pltpu.make_async_copy(f_hbm.at[r], f.at[k], rest_sem.at[k, 2]),
            pltpu.make_async_copy(c_hbm.at[r], c.at[k], rest_sem.at[k, 3]),
        ]
    if halo:
        for k, dst in enumerate((u, v)):
            halo_copies.append(
                pltpu.make_async_copy(low_hbm.at[k], dst.at[:, pl.ds(0, 2)], halo_sem.at[0, k])
            )
            halo_copies.append(
                pltpu.make_async_copy(
                    high_hbm.at[k], dst.at[:, pl.ds(extended - 2, 2)], halo_sem.at[1, k]
                )
            )
    for copy in halo_copies:
        copy.start()
    for r in own:
        for copy in wind_copies[r]:
            copy.start()
        if r in rows:
            for copy in rest_copies[rows.index(r)]:
                copy.start()
    if halo:
        moment_ref[...] = start_ref[...]
    else:
        moment_ref[...] = jnp.zeros_like(moment_ref)
    for copy in halo_copies:
        copy.wait()
    waited = set()
    for k, r in enumerate(rows):
        for d in range(-2, 3):
            if r + d in wind_copies and r + d not in waited:
                waited.add(r + d)
                for copy in wind_copies[r + d]:
                    copy.wait()
        for copy in rest_copies[k]:
            copy.wait()
        e = r + 2
        for m in range(members):
            both = jnp.concatenate([v[m, e], u[m, e]], axis=1)
            dlon[m] = jnp.dot(shift_ref[...], both, preferred_element_type=jnp.float32)

        def chunk(j, carry):
            at = pl.ds(pl.multiple_of(j * CHUNK, CHUNK), CHUNK)
            factor = f[k, at, :]
            curl_factor = c[k, at, :]
            slope = slope_ref[...]
            held, total = [], None
            for m in range(members):
                def wind(ref, d):
                    return ref[m, e + d, at, :].astype(jnp.float32)

                def lat(ref):
                    return 8.0 * (wind(ref, 1) - wind(ref, -1)) - (wind(ref, 2) - wind(ref, -2))

                curl = factor * (dlon[m, at, :levels] - lat(u))
                spread = factor * (dlon[m, at, levels:] + lat(v))
                heat = h[k, m, at, :].astype(jnp.float32) - curl_factor * curl
                moist = q[k, m, at, :].astype(jnp.float32) - slope * heat
                state = (curl, spread, heat, moist)
                held.append(state)
                total = state if total is None else tuple(a + b for a, b in zip(total, state))
            mean = tuple(a * (1.0 / members) for a in total)
            for n in range(4):
                lanes = slice(n * levels, (n + 1) * levels)
                mean_ref[k, at, lanes] = mean[n].astype(jnp.bfloat16)
                for m in range(members):
                    anom[m, at, lanes] = (held[m][n] - mean[n]).astype(jnp.bfloat16)
            return carry

        lax.fori_loop(0, lons // CHUNK, chunk, 0)
        for m in range(members):
            a = anom[m]
            moment_ref[...] += lax.dot_general(
                a, a, (((0,), (0,)), ((), ())), preferred_element_type=jnp.float32
            )


def moments(rows, fields, factors, shift, slope, halos=None, start=None):
    members, height, lons, levels = fields[0].shape
    count, width = len(rows), 4 * levels
    halo = halos is not None
    hbm = pl.BlockSpec(memory_space=pl.ANY)
    vmem = pl.BlockSpec(memory_space=pltpu.VMEM)
    operands = list(fields) + list(factors)
    specs = [hbm] * 6
    if halo:
        operands += list(halos) + [start]
        specs += [hbm, hbm, vmem]
    operands += [shift, slope]
    specs += [vmem, vmem]
    bf16, f32 = jnp.bfloat16, jnp.float32
    return pl.pallas_call(
        functools.partial(moments_kernel, rows, halo),
        out_shape=(
            jax.ShapeDtypeStruct((count, lons, width), bf16),
            jax.ShapeDtypeStruct((width, width), f32),
        ),
        in_specs=specs,
        out_specs=(vmem, vmem),
        scratch_shapes=[
            pltpu.VMEM((members, height + 4, lons, levels), bf16),
            pltpu.VMEM((members, height + 4, lons, levels), bf16),
            pltpu.VMEM((count, members, lons, levels), bf16),
            pltpu.VMEM((count, members, lons, levels), bf16),
            pltpu.VMEM((count, lons, levels), f32),
            pltpu.VMEM((count, lons, levels), f32),
            pltpu.VMEM((members, lons, 2 * levels), f32),
            pltpu.VMEM((members, lons, width), bf16),
            pltpu.SemaphoreType.DMA((height, 2)),
            pltpu.SemaphoreType.DMA((count, 4)),
            pltpu.SemaphoreType.DMA((2, 2)),
        ],
        compiler_params=pltpu.CompilerParams(vmem_limit_bytes=40 * 2**20),
        cost_estimate=pl.CostEstimate(
            flops=2 * count * members * lons * width * width * 2,
            bytes_accessed=12 * 2**20,
            transcendentals=0,
        ),
        name="halo_moments" if halo else "inner_moments",
    )(*operands)


def edge_rows(winds, axis):
    count = lax.axis_size(axis)
    forward = [(i, i + 1) for i in range(count - 1)]
    backward = [(b, a) for a, b in forward]
    low = jnp.stack([w[:, -2:] for w in winds])
    high = jnp.stack([w[:, :2] for w in winds])
    return lax.ppermute(low, axis, forward), lax.ppermute(high, axis, backward)


def shares(whole, axis):
    count = lax.axis_size(axis)
    me = lax.axis_index(axis)
    size = whole.shape[0] // count
    got = [lax.dynamic_slice_in_dim(whole, me * size, size, 0)]
    for k in range(1, count):
        target = me ^ k
        block = lax.dynamic_slice_in_dim(whole, target * size, size, 0)
        got.append(lax.ppermute(block, axis, [(i, i ^ k) for i in range(count)]))
    return got


def between(means, axis):
    got = jnp.stack(shares(means.reshape(-1, means.shape[-1]), axis)).astype(jnp.float32)
    away = (got - jnp.mean(got, axis=0, keepdims=True)).astype(jnp.bfloat16)
    return away.reshape(-1, away.shape[-1])


def on_device(u, v, h, q, projection_scale, balance_multiplier, heat_slope, moist_slope):
    members, height, lons, levels = u.shape
    groups = lax.axis_size("member")
    scale = 1.0 / ((members * groups - 1) * height * lons)
    shape = (height, lons, levels)
    factor = jnp.broadcast_to((projection_scale / 12.0)[:, :, None], shape)
    curl_factor = balance_multiplier[:, :, None] * heat_slope
    eye = jnp.eye(lons, dtype=jnp.bfloat16)
    shift = 6.0 * (jnp.roll(eye, 1, 1) - jnp.roll(eye, -1, 1))
    slope = moist_slope[None]
    fields, factors = (u, v, h, q), (factor, curl_factor)
    halos = edge_rows((u, v), "space")
    inner = tuple(range(2, height - 2))
    outer = (0, 1, height - 2, height - 1)
    inner_mean, start = moments(inner, fields, factors, shift, slope)
    inner_away = between(inner_mean, "member")
    outer_mean, moment = moments(outer, fields, factors, shift, slope, halos, start)
    outer_away = between(outer_mean, "member")
    away = jnp.concatenate([inner_away, outer_away])
    moment += members * lax.dot_general(
        away, away, (((0,), (0,)), ((), ())), preferred_element_type=jnp.float32
    )
    return (sum(shares(moment, "member")) * scale)[None]


def solution(mesh):
    placed = (
        P("member", "space", None, None),
        P("member", "space", None, None),
        P("member", "space", None, None),
        P("member", "space", None, None),
        P("space", None),
        P("space", None),
        P(),
        P(),
    )
    return jax.shard_map(
        on_device, mesh=mesh, in_specs=placed, out_specs=P("space", "member", None), check_vma=False
    )
```

```python
import jax
import jax.numpy as jnp
from jax import lax
from jax.experimental import pallas as pl
from jax.experimental.pallas import tpu as pltpu
from jax.sharding import PartitionSpec as P

CHUNK = 16
LAG = 3
MESH = pl.DeviceIdType.MESH
BF16, F32 = jnp.bfloat16, jnp.float32


def kernel(
    groups, bands, scale, u_hbm, v_hbm, h_hbm, q_hbm, f_hbm, c_hbm, shift_ref, slope_ref, out_ref,
    u, v, h, q, f, c, dlon, anom, mean_rows, got, moment, parts,
    wind_sem, rest_sem, halo_send, halo_recv, mean_send, mean_recv, part_send, part_recv,
):
    members, extended, lons, levels = u.shape
    height = extended - 4
    share = lons // groups
    block = moment.shape[0] // groups
    me = lax.axis_index("member")
    band = lax.axis_index("space")
    has_low, has_high = band > 0, band < bands - 1
    even = lax.rem(band, 2) == 0

    def target(j):
        return lax.rem(me + j, groups)

    def wind_copies(r):
        return [
            pltpu.make_async_copy(u_hbm.at[:, r], u.at[:, r + 2], wind_sem.at[r, 0]),
            pltpu.make_async_copy(v_hbm.at[:, r], v.at[:, r + 2], wind_sem.at[r, 1]),
        ]

    def rest_copies(r):
        return [
            pltpu.make_async_copy(h_hbm.at[:, r], h.at[:, r], rest_sem.at[r, 0]),
            pltpu.make_async_copy(q_hbm.at[:, r], q.at[:, r], rest_sem.at[r, 1]),
            pltpu.make_async_copy(f_hbm.at[r], f.at[r], rest_sem.at[r, 2]),
            pltpu.make_async_copy(c_hbm.at[r], c.at[r], rest_sem.at[r, 3]),
        ]

    def halo_copies(up):
        here = height - 2 if up else 0
        there = 0 if up else height + 2
        to = band + 1 if up else band - 1
        return [
            pltpu.make_async_remote_copy(
                src_ref=src.at[:, pl.ds(here, 2)],
                dst_ref=dst.at[:, pl.ds(there, 2)],
                send_sem=halo_send.at[int(up), k],
                recv_sem=halo_recv.at[int(up), k],
                device_id={"space": to},
                device_id_type=MESH,
            )
            for k, (src, dst) in enumerate(((u_hbm, u), (v_hbm, v)))
        ]

    def mean_copy(j, k):
        at = pl.ds(pl.multiple_of(target(j) * share, share), share)
        return pltpu.make_async_remote_copy(
            src_ref=mean_rows.at[k, at],
            dst_ref=got.at[k, j - 1],
            send_sem=mean_send.at[k, j - 1],
            recv_sem=mean_recv.at[k, j - 1],
            device_id={"member": target(j)},
            device_id_type=MESH,
        )

    def part_copy(j):
        at = pl.ds(pl.multiple_of(target(j) * block, block), block)
        return pltpu.make_async_remote_copy(
            src_ref=moment.at[at],
            dst_ref=parts.at[j - 1],
            send_sem=part_send.at[j - 1],
            recv_sem=part_recv.at[j - 1],
            device_id={"member": target(j)},
            device_id_type=MESH,
        )

    def row_of(k):
        first = jnp.where(even, height - 2, 0)
        second = jnp.where(even, 0, height - 2)
        inner = height - 4
        return jnp.where(k < inner, k + 2, jnp.where(k < inner + 2, first + k - inner, second + k - inner - 2))

    barrier = pltpu.get_barrier_semaphore()
    for j in range(1, groups):
        pl.semaphore_signal(barrier, inc=1, device_id={"member": target(j)}, device_id_type=MESH)

    @pl.when(has_low)
    def _():
        pl.semaphore_signal(barrier, inc=1, device_id={"space": band - 1}, device_id_type=MESH)

    @pl.when(has_high)
    def _():
        pl.semaphore_signal(barrier, inc=1, device_id={"space": band + 1}, device_id_type=MESH)

    def start_row(r, carry):
        for copy in wind_copies(r):
            copy.start()
        return carry

    def start_rest(k, carry):
        for copy in rest_copies(row_of(k)):
            copy.start()
        return carry

    lax.fori_loop(0, 5, start_row, 0)
    lax.fori_loop(0, 1, start_rest, 0)

    pl.semaphore_wait(barrier, groups - 1 + has_low.astype(jnp.int32) + has_high.astype(jnp.int32))

    @pl.when(has_low)
    def _():
        for copy in halo_copies(False):
            copy.start()

    @pl.when(has_high)
    def _():
        for copy in halo_copies(True):
            copy.start()

    lax.fori_loop(5, height, start_row, 0)
    lax.fori_loop(1, height, start_rest, 0)

    moment[...] = jnp.zeros_like(moment)

    @pl.when(jnp.logical_not(has_low))
    def _():
        u[:, pl.ds(0, 2)] = jnp.zeros((members, 2, lons, levels), BF16)
        v[:, pl.ds(0, 2)] = jnp.zeros((members, 2, lons, levels), BF16)

    @pl.when(jnp.logical_not(has_high))
    def _():
        u[:, pl.ds(height + 2, 2)] = jnp.zeros((members, 2, lons, levels), BF16)
        v[:, pl.ds(height + 2, 2)] = jnp.zeros((members, 2, lons, levels), BF16)

    def receive_low():
        for copy in halo_copies(True):
            copy.wait_recv()

    def receive_high():
        for copy in halo_copies(False):
            copy.wait_recv()

    def wait_row(r, carry):
        for copy in wind_copies(r):
            copy.wait()
        return carry

    lax.fori_loop(0, 4, wait_row, 0)

    def between(k, carry):
        for j in range(1, groups):
            mean_copy(j, k).wait_recv()
        at = pl.ds(pl.multiple_of(me * share, share), share)
        each = [mean_rows[k, at].astype(F32)]
        each += [got[k, j].astype(F32) for j in range(groups - 1)]
        mean = sum(each[1:], each[0]) * (1.0 / groups)
        away = jnp.concatenate([a - mean for a in each], axis=0).astype(BF16)
        moment[...] += members * lax.dot_general(
            away, away, (((0,), (0,)), ((), ())), preferred_element_type=F32
        )
        return carry

    def row(k, carry):
        r = row_of(k)
        e = r + 2
        inner = height - 4

        @pl.when(k < inner)
        def _():
            wait_row(k + 4, 0)

        @pl.when((k == inner) & even & has_high | (k == inner + 2) & jnp.logical_not(even) & has_high)
        def _():
            receive_high()

        @pl.when((k == inner + 2) & even & has_low | (k == inner) & jnp.logical_not(even) & has_low)
        def _():
            receive_low()

        for copy in rest_copies(r):
            copy.wait()
        for m in range(members):
            both = jnp.concatenate([v[m, e], u[m, e]], axis=1)
            dlon[m] = jnp.dot(shift_ref[...], both, preferred_element_type=F32)

        def chunk(i, carry):
            at = pl.ds(pl.multiple_of(i * CHUNK, CHUNK), CHUNK)
            factor = f[r, at, :]
            curl_factor = c[r, at, :]
            slope = slope_ref[...]
            held, total = [], None
            for m in range(members):

                def wind(ref, d):
                    return ref[m, e + d, at, :].astype(F32)

                def lat(ref):
                    return 8.0 * (wind(ref, 1) - wind(ref, -1)) - (wind(ref, 2) - wind(ref, -2))

                curl = factor * (dlon[m, at, :levels] - lat(u))
                spread = factor * (dlon[m, at, levels:] + lat(v))
                heat = h[m, r, at, :].astype(F32) - curl_factor * curl
                moist = q[m, r, at, :].astype(F32) - slope * heat
                state = (curl, spread, heat, moist)
                held.append(state)
                total = state if total is None else tuple(a + b for a, b in zip(total, state))
            mean = tuple(a * (1.0 / members) for a in total)
            for n in range(4):
                lanes = slice(n * levels, (n + 1) * levels)
                mean_rows[k, at, lanes] = mean[n].astype(BF16)
                for m in range(members):
                    to = pl.ds(pl.multiple_of(m * lons + i * CHUNK, CHUNK), CHUNK)
                    anom[to, lanes] = (held[m][n] - mean[n]).astype(BF16)
            return carry

        lax.fori_loop(0, lons // CHUNK, chunk, 0)
        for j in range(1, groups):
            mean_copy(j, k).start()
        a = anom[...]
        moment[...] += lax.dot_general(a, a, (((0,), (0,)), ((), ())), preferred_element_type=F32)

        @pl.when(k >= LAG)
        def _():
            between(k - LAG, 0)

        return carry

    lax.fori_loop(0, height, row, 0)
    lax.fori_loop(height - LAG, height, between, 0)
    for j in range(1, groups):
        part_copy(j).start()
    total = moment[pl.ds(pl.multiple_of(me * block, block), block), :]
    for j in range(1, groups):
        part_copy(j).wait_recv()
        total += parts[j - 1]
    out_ref[...] = total * scale

    def sent(k, carry):
        for j in range(1, groups):
            mean_copy(j, k).wait_send()
        return carry

    lax.fori_loop(0, height, sent, 0)
    for j in range(1, groups):
        part_copy(j).wait_send()

    @pl.when(has_low)
    def _():
        for copy in halo_copies(False):
            copy.wait_send()

    @pl.when(has_high)
    def _():
        for copy in halo_copies(True):
            copy.wait_send()


def on_device(u, v, h, q, projection_scale, balance_multiplier, heat_slope, moist_slope):
    members, height, lons, levels = u.shape
    groups = lax.axis_size("member")
    bands = lax.axis_size("space")
    width = 4 * levels
    scale = 1.0 / ((members * groups - 1) * height * lons)
    shape = (height, lons, levels)
    factor = jnp.broadcast_to((projection_scale / 12.0)[:, :, None], shape)
    curl_factor = balance_multiplier[:, :, None] * heat_slope
    j = lax.broadcasted_iota(jnp.int32, (lons, lons), 0)
    i = lax.broadcasted_iota(jnp.int32, (lons, lons), 1)
    ahead = lax.rem(i - j + lons, lons)
    shift = jnp.where(ahead == 1, 6.0, jnp.where(ahead == lons - 1, -6.0, 0.0)).astype(BF16)
    slope = moist_slope[None]
    share, block, others = lons // groups, width // groups, groups - 1
    hbm = pl.BlockSpec(memory_space=pl.ANY)
    vmem = pl.BlockSpec(memory_space=pltpu.VMEM)
    dma = pltpu.SemaphoreType.DMA

    def body(*refs):
        kernel(groups, bands, scale, *refs)

    out = pl.pallas_call(
        body,
        out_shape=jax.ShapeDtypeStruct((block, width), F32),
        in_specs=[hbm] * 6 + [vmem] * 2,
        out_specs=vmem,
        scratch_shapes=[
            pltpu.VMEM((members, height + 4, lons, levels), BF16),
            pltpu.VMEM((members, height + 4, lons, levels), BF16),
            pltpu.VMEM((members, height, lons, levels), BF16),
            pltpu.VMEM((members, height, lons, levels), BF16),
            pltpu.VMEM(shape, F32),
            pltpu.VMEM(shape, F32),
            pltpu.VMEM((members, lons, 2 * levels), F32),
            pltpu.VMEM((members * lons, width), BF16),
            pltpu.VMEM((height, lons, width), BF16),
            pltpu.VMEM((height, others, share, width), BF16),
            pltpu.VMEM((width, width), F32),
            pltpu.VMEM((others, block, width), F32),
            dma((height, 2)),
            dma((height, 4)),
            dma((2, 2)),
            dma((2, 2)),
            dma((height, others)),
            dma((height, others)),
            dma((others,)),
            dma((others,)),
        ],
        compiler_params=pltpu.CompilerParams(
            collective_id=0, has_side_effects=True, vmem_limit_bytes=56 * 2**20
        ),
        cost_estimate=pl.CostEstimate(
            flops=2 * members * height * lons * width * width,
            bytes_accessed=16 * 2**20,
            transcendentals=0,
        ),
        name="band_moments",
    )(u, v, h, q, factor, curl_factor, shift, slope)
    return out[None]


def solution(mesh):
    placed = (
        P("member", "space", None, None),
        P("member", "space", None, None),
        P("member", "space", None, None),
        P("member", "space", None, None),
        P("space", None),
        P("space", None),
        P(),
        P(),
    )
    return jax.shard_map(
        on_device, mesh=mesh, in_specs=placed, out_specs=P("space", "member", None), check_vma=False
    )
```

```python
import functools

import jax
import jax.numpy as jnp
from jax import lax
from jax.experimental import pallas as pl
from jax.experimental.pallas import tpu as pltpu
from jax.sharding import PartitionSpec as P

CHUNK = 16
LAG = 3
MESH = pl.DeviceIdType.MESH
BF16, F32 = jnp.bfloat16, jnp.float32


def kernel(
    groups, bands, u_hbm, v_hbm, h_hbm, q_hbm, scale_ref, balance_ref, heat_slope_ref, slope_ref, out_ref,
    u, v, h, q, f, c, shift, dlon_a, dlon_b, anom_a, anom_b, mean_rows, got, moment, parts,
    wind_sem, rest_sem, halo_send, halo_recv, mean_send, mean_recv, part_send, part_recv,
):
    members, extended, lons, levels = u.shape
    height = extended - 4
    half = lons // 2
    share = lons // groups
    block = moment.shape[0] // groups
    me = lax.axis_index("member")
    band = lax.axis_index("space")
    has_low, has_high = band > 0, band < bands - 1
    even = lax.rem(band, 2) == 0

    def target(j):
        return lax.rem(me + j, groups)

    def wind_copies(r):
        return [
            pltpu.make_async_copy(u_hbm.at[:, r], u.at[:, r + 2], wind_sem.at[r, 0]),
            pltpu.make_async_copy(v_hbm.at[:, r], v.at[:, r + 2], wind_sem.at[r, 1]),
        ]

    def rest_copies(r):
        return [
            pltpu.make_async_copy(h_hbm.at[:, r], h.at[:, r], rest_sem.at[r, 0]),
            pltpu.make_async_copy(q_hbm.at[:, r], q.at[:, r], rest_sem.at[r, 1]),
        ]

    def halo_copies(up):
        here = height - 2 if up else 0
        there = 0 if up else height + 2
        to = band + 1 if up else band - 1
        return [
            pltpu.make_async_remote_copy(
                src_ref=src.at[:, pl.ds(here, 2)],
                dst_ref=dst.at[:, pl.ds(there, 2)],
                send_sem=halo_send.at[int(up), k],
                recv_sem=halo_recv.at[int(up), k],
                device_id={"space": to},
                device_id_type=MESH,
            )
            for k, (src, dst) in enumerate(((u_hbm, u), (v_hbm, v)))
        ]

    def mean_copy(j, k):
        at = pl.ds(pl.multiple_of(target(j) * share, share), share)
        return pltpu.make_async_remote_copy(
            src_ref=mean_rows.at[k, at],
            dst_ref=got.at[k, j - 1],
            send_sem=mean_send.at[k, j - 1],
            recv_sem=mean_recv.at[k, j - 1],
            device_id={"member": target(j)},
            device_id_type=MESH,
        )

    def part_copy(j):
        at = pl.ds(pl.multiple_of(target(j) * block, block), block)
        return pltpu.make_async_remote_copy(
            src_ref=moment.at[at],
            dst_ref=parts.at[j - 1],
            send_sem=part_send.at[j - 1],
            recv_sem=part_recv.at[j - 1],
            device_id={"member": target(j)},
            device_id_type=MESH,
        )

    def row_of(k):
        first = jnp.where(even, height - 2, 0)
        second = jnp.where(even, 0, height - 2)
        inner = height - 4
        return jnp.where(k < inner, k + 2, jnp.where(k < inner + 2, first + k - inner, second + k - inner - 2))

    barrier = pltpu.get_barrier_semaphore()
    for j in range(1, groups):
        pl.semaphore_signal(barrier, inc=1, device_id={"member": target(j)}, device_id_type=MESH)

    @pl.when(has_low)
    def _():
        pl.semaphore_signal(barrier, inc=1, device_id={"space": band - 1}, device_id_type=MESH)

    @pl.when(has_high)
    def _():
        pl.semaphore_signal(barrier, inc=1, device_id={"space": band + 1}, device_id_type=MESH)

    def start_row(r, carry):
        for copy in wind_copies(r):
            copy.start()
        return carry

    def start_rest(k, carry):
        for copy in rest_copies(row_of(k)):
            copy.start()
        return carry

    lax.fori_loop(0, 5, start_row, 0)
    lax.fori_loop(0, 1, start_rest, 0)

    pl.semaphore_wait(barrier, groups - 1 + has_low.astype(jnp.int32) + has_high.astype(jnp.int32))

    @pl.when(has_low)
    def _():
        for copy in halo_copies(False):
            copy.start()

    @pl.when(has_high)
    def _():
        for copy in halo_copies(True):
            copy.start()

    lax.fori_loop(5, height, start_row, 0)
    lax.fori_loop(1, height, start_rest, 0)

    moment[...] = jnp.zeros_like(moment)
    anom_b[...] = jnp.zeros_like(anom_b)
    here = lax.broadcasted_iota(jnp.int32, (lons, lons), 0)
    there = lax.broadcasted_iota(jnp.int32, (lons, lons), 1)
    ahead = there - here
    right = (ahead == 1) | (ahead == 1 - lons)
    left = (ahead == -1) | (ahead == lons - 1)
    shift[...] = jnp.where(right, 6.0, jnp.where(left, -6.0, 0.0)).astype(BF16)

    def factors(r, carry):
        def spread(ref):
            return jnp.broadcast_to(ref[pl.ds(r, 1), :], (levels, lons)).T

        f[r] = spread(scale_ref) * (1.0 / 12.0)
        c[r] = spread(balance_ref) * heat_slope_ref[...]
        return carry

    lax.fori_loop(0, height, factors, 0)

    @pl.when(jnp.logical_not(has_low))
    def _():
        u[:, pl.ds(0, 2)] = jnp.zeros((members, 2, lons, levels), BF16)
        v[:, pl.ds(0, 2)] = jnp.zeros((members, 2, lons, levels), BF16)

    @pl.when(jnp.logical_not(has_high))
    def _():
        u[:, pl.ds(height + 2, 2)] = jnp.zeros((members, 2, lons, levels), BF16)
        v[:, pl.ds(height + 2, 2)] = jnp.zeros((members, 2, lons, levels), BF16)

    def receive_low():
        for copy in halo_copies(True):
            copy.wait_recv()

    def receive_high():
        for copy in halo_copies(False):
            copy.wait_recv()

    def wait_row(r, carry):
        for copy in wind_copies(r):
            copy.wait()
        return carry

    lax.fori_loop(0, 4, wait_row, 0)

    def gram(a, times):
        cut = a.shape[1] // 2
        top = lax.dot_general(
            a[:, :cut], a, (((0,), (0,)), ((), ())), preferred_element_type=F32
        )
        low = lax.dot_general(
            a[:, cut:], a[:, cut:], (((0,), (0,)), ((), ())), preferred_element_type=F32
        )
        moment[:cut, :] += top if times == 1 else times * top
        moment[cut:, cut:] += low if times == 1 else times * low

    def longitude(dlon, e, side):
        at = slice(side * half, (side + 1) * half)
        for m in range(members):
            both = jnp.concatenate([v[m, e], u[m, e]], axis=1)
            dlon[m] = jnp.dot(shift[at, :], both, preferred_element_type=F32)

    def between(k, carry):
        for j in range(1, groups):
            mean_copy(j, k).wait_recv()
        at = pl.ds(pl.multiple_of(me * share, share), share)
        each = [mean_rows[k, at].astype(F32)]
        each += [got[k, j].astype(F32) for j in range(groups - 1)]
        mean = sum(each[1:], each[0]) * (1.0 / groups)
        away = jnp.concatenate([a - mean for a in each], axis=0).astype(BF16)
        gram(away, members)
        return carry

    def row(k, carry):
        r = row_of(k)
        e = r + 2
        inner = height - 4

        @pl.when(k < inner)
        def _():
            wait_row(k + 4, 0)

        @pl.when((k == inner) & even & has_high | (k == inner + 2) & jnp.logical_not(even) & has_high)
        def _():
            receive_high()

        @pl.when((k == inner + 2) & even & has_low | (k == inner) & jnp.logical_not(even) & has_low)
        def _():
            receive_low()

        for copy in rest_copies(r):
            copy.wait()
        def chunk(side, dlon, anom, i, carry):
            within = pl.ds(pl.multiple_of(i * CHUNK, CHUNK), CHUNK)
            at = pl.ds(pl.multiple_of(side * half + i * CHUNK, CHUNK), CHUNK)
            factor = f[r, at, :]
            curl_factor = c[r, at, :]
            slope = slope_ref[...]
            held, total = [], None
            for m in range(members):

                def wind(ref, d):
                    return ref[m, e + d, at, :].astype(F32)

                def lat(ref):
                    return 8.0 * (wind(ref, 1) - wind(ref, -1)) - (wind(ref, 2) - wind(ref, -2))

                curl = factor * (dlon[m, within, :levels] - lat(u))
                spread = factor * (dlon[m, within, levels:] + lat(v))
                heat = h[m, r, at, :].astype(F32) - curl_factor * curl
                moist = q[m, r, at, :].astype(F32) - slope * heat
                state = (curl, spread, heat, moist)
                held.append(state)
                total = state if total is None else tuple(a + b for a, b in zip(total, state))
            mean = tuple(a * (1.0 / members) for a in total)
            for n in range(4):
                lanes = slice(n * levels, (n + 1) * levels)
                mean_rows[k, at, lanes] = mean[n].astype(BF16)
                for m in range(members):
                    to = pl.ds(pl.multiple_of(m * half + i * CHUNK, CHUNK), CHUNK)
                    anom[to, lanes] = (held[m][n] - mean[n]).astype(BF16)
            return carry

        steps = half // CHUNK
        gram(anom_b[...], 1)
        longitude(dlon_b, e, 1)
        lax.fori_loop(0, steps, functools.partial(chunk, 0, dlon_a, anom_a), 0, unroll=True)
        gram(anom_a[...], 1)
        longitude(dlon_a, row_of(jnp.minimum(k + 1, height - 1)) + 2, 0)
        lax.fori_loop(0, steps, functools.partial(chunk, 1, dlon_b, anom_b), 0, unroll=True)
        for j in range(1, groups):
            mean_copy(j, k).start()

        @pl.when(k >= LAG)
        def _():
            between(k - LAG, 0)

        return carry

    longitude(dlon_a, row_of(0) + 2, 0)
    lax.fori_loop(0, height, row, 0)
    gram(anom_b[...], 1)
    lax.fori_loop(height - LAG, height, between, 0)
    cut = moment.shape[0] // 2
    moment[cut:, :cut] = moment[:cut, cut:].T
    for j in range(1, groups):
        part_copy(j).start()
    total = moment[pl.ds(pl.multiple_of(me * block, block), block), :]
    for j in range(1, groups):
        part_copy(j).wait_recv()
        total += parts[j - 1]
    out_ref[...] = total

    def sent(k, carry):
        for j in range(1, groups):
            mean_copy(j, k).wait_send()
        return carry

    lax.fori_loop(0, height, sent, 0)
    for j in range(1, groups):
        part_copy(j).wait_send()

    @pl.when(has_low)
    def _():
        for copy in halo_copies(False):
            copy.wait_send()

    @pl.when(has_high)
    def _():
        for copy in halo_copies(True):
            copy.wait_send()


def on_device(u, v, h, q, projection_scale, balance_multiplier, heat_slope, moist_slope):
    members, height, lons, levels = u.shape
    groups = lax.axis_size("member")
    bands = lax.axis_size("space")
    width = 4 * levels
    scale = 1.0 / ((members * groups - 1) * height * lons)
    shape = (height, lons, levels)
    share, block, others = lons // groups, width // groups, groups - 1
    hbm = pl.BlockSpec(memory_space=pl.ANY)
    vmem = pl.BlockSpec(memory_space=pltpu.VMEM)
    dma = pltpu.SemaphoreType.DMA

    def body(*refs):
        kernel(groups, bands, *refs)

    out = pl.pallas_call(
        body,
        out_shape=jax.ShapeDtypeStruct((block, width), F32),
        in_specs=[hbm] * 4 + [vmem] * 4,
        out_specs=vmem,
        scratch_shapes=[
            pltpu.VMEM((members, height + 4, lons, levels), BF16),
            pltpu.VMEM((members, height + 4, lons, levels), BF16),
            pltpu.VMEM((members, height, lons, levels), BF16),
            pltpu.VMEM((members, height, lons, levels), BF16),
            pltpu.VMEM(shape, F32),
            pltpu.VMEM(shape, F32),
            pltpu.VMEM((lons, lons), BF16),
            pltpu.VMEM((members, lons // 2, 2 * levels), F32),
            pltpu.VMEM((members, lons // 2, 2 * levels), F32),
            pltpu.VMEM((members * lons // 2, width), BF16),
            pltpu.VMEM((members * lons // 2, width), BF16),
            pltpu.VMEM((height, lons, width), BF16),
            pltpu.VMEM((height, others, share, width), BF16),
            pltpu.VMEM((width, width), F32),
            pltpu.VMEM((others, block, width), F32),
            dma((height, 2)),
            dma((height, 2)),
            dma((2, 2)),
            dma((2, 2)),
            dma((height, others)),
            dma((height, others)),
            dma((others,)),
            dma((others,)),
        ],
        compiler_params=pltpu.CompilerParams(
            collective_id=0, has_side_effects=True, vmem_limit_bytes=56 * 2**20
        ),
        cost_estimate=pl.CostEstimate(
            flops=2 * members * height * lons * width * width,
            bytes_accessed=16 * 2**20,
            transcendentals=0,
        ),
        name="band_moments",
    )(u, v, h, q, projection_scale, balance_multiplier, heat_slope[None], moist_slope[None])
    return (out * scale)[None]


def solution(mesh):
    placed = (
        P("member", "space", None, None),
        P("member", "space", None, None),
        P("member", "space", None, None),
        P("member", "space", None, None),
        P("space", None),
        P("space", None),
        P(),
        P(),
    )
    return jax.shard_map(
        on_device, mesh=mesh, in_specs=placed, out_specs=P("space", "member", None), check_vma=False
    )
```

```python
import functools
import itertools

import jax
import jax.numpy as jnp
from jax import lax
from jax.experimental import pallas as pl
from jax.experimental.pallas import tpu as pltpu
from jax.sharding import PartitionSpec as P

CHUNK = 16
MESH = pl.DeviceIdType.MESH
BF16, F32 = jnp.bfloat16, jnp.float32


def kernel(
    groups, bands, u_hbm, v_hbm, h_hbm, q_hbm, scale_ref, balance_ref, heat_slope_ref, slope_ref, out_ref,
    u, v, h, q, f, c, shift, dlon_a, dlon_b, anom_a, anom_b, mean_rows, got, kept, away, moment, parts,
    wind_sem, rest_sem, halo_send, halo_recv, mean_send, mean_recv, part_send, part_recv,
):
    members, extended, lons, levels = u.shape
    height = extended - 4
    half = lons // 2
    width = moment.shape[1]
    block = width // groups
    bits = groups.bit_length() - 1
    orders = (tuple(range(bits)), tuple(reversed(range(bits))))
    columns = width // 2
    sizes = [lons // 2 ** (t + 2) for t in range(bits)]
    starts = [2 * sum(sizes[:t]) for t in range(bits)]
    me = lax.axis_index("member")
    band = lax.axis_index("space")
    has_low, has_high = band > 0, band < bands - 1
    even = lax.rem(band, 2) == 0

    def bit(b):
        return lax.rem(lax.div(me, 2**b), 2)

    def partner(b):
        return me + (1 - 2 * bit(b)) * 2**b

    def wind_copies(r):
        return [
            pltpu.make_async_copy(u_hbm.at[:, r], u.at[:, r + 2], wind_sem.at[r, 0]),
            pltpu.make_async_copy(v_hbm.at[:, r], v.at[:, r + 2], wind_sem.at[r, 1]),
        ]

    def rest_copies(r):
        return [
            pltpu.make_async_copy(h_hbm.at[:, r], h.at[:, r], rest_sem.at[r, 0]),
            pltpu.make_async_copy(q_hbm.at[:, r], q.at[:, r], rest_sem.at[r, 1]),
        ]

    def halo_copies(up):
        here = height - 2 if up else 0
        there = 0 if up else height + 2
        to = band + 1 if up else band - 1
        return [
            pltpu.make_async_remote_copy(
                src_ref=src.at[:, pl.ds(here, 2)],
                dst_ref=dst.at[:, pl.ds(there, 2)],
                send_sem=halo_send.at[int(up), k],
                recv_sem=halo_recv.at[int(up), k],
                device_id={"space": to},
                device_id_type=MESH,
            )
            for k, (src, dst) in enumerate(((u_hbm, u), (v_hbm, v)))
        ]

    def piece(t, stream, k, keep):
        b = bit(orders[stream][t])
        b = b if keep else 1 - b
        size = sizes[t]
        if t == 0:
            at = pl.multiple_of(stream * half + b * size, size)
            return mean_rows.at[k, pl.ds(at, size)]
        at = pl.multiple_of(starts[t - 1] + stream * sizes[t - 1] + b * size, size)
        return kept.at[k, pl.ds(at, size)]

    def mean_copy(t, stream, k):
        return pltpu.make_async_remote_copy(
            src_ref=piece(t, stream, k, False),
            dst_ref=got.at[k, pl.ds(starts[t] + stream * sizes[t], sizes[t])],
            send_sem=mean_send.at[k, t, stream],
            recv_sem=mean_recv.at[k, t, stream],
            device_id={"member": partner(orders[stream][t])},
            device_id_type=MESH,
        )

    def flips(t):
        return list(itertools.product((1, 0), repeat=bits - 1 - t))

    def part_view(t, stream, flip, keep):
        order = orders[stream]
        owner = 0
        for place, b in enumerate(order):
            other = (not keep) if place == t else place > t and flip[place - t - 1]
            owner = owner + (1 - bit(b) if other else bit(b)) * 2**b
        return moment.at[
            pl.ds(pl.multiple_of(owner * block, block), block), pl.ds(stream * columns, columns)
        ]

    def slot(t, flip):
        return sum(2 ** (bits - 1 - x) for x in range(t)) + flips(t).index(flip)

    def part_copy(t, stream, flip):
        n = slot(t, flip)
        return pltpu.make_async_remote_copy(
            src_ref=part_view(t, stream, flip, False),
            dst_ref=parts.at[stream, n],
            send_sem=part_send.at[stream, n],
            recv_sem=part_recv.at[stream, n],
            device_id={"member": partner(orders[stream][t])},
            device_id_type=MESH,
        )

    def take(t, stream, flip):
        part_copy(t, stream, flip).wait_recv()
        view = part_view(t, stream, flip, True)
        view[...] += parts[stream, slot(t, flip)]

    def row_of(k):
        first = jnp.where(even, height - 2, 0)
        second = jnp.where(even, 0, height - 2)
        inner = height - 4
        return jnp.where(k < inner, k + 2, jnp.where(k < inner + 2, first + k - inner, second + k - inner - 2))

    barrier = pltpu.get_barrier_semaphore()
    for b in range(bits):
        pl.semaphore_signal(barrier, inc=1, device_id={"member": partner(b)}, device_id_type=MESH)

    @pl.when(has_low)
    def _():
        pl.semaphore_signal(barrier, inc=1, device_id={"space": band - 1}, device_id_type=MESH)

    @pl.when(has_high)
    def _():
        pl.semaphore_signal(barrier, inc=1, device_id={"space": band + 1}, device_id_type=MESH)

    def start_row(r, carry):
        for copy in wind_copies(r):
            copy.start()
        return carry

    def start_rest(k, carry):
        for copy in rest_copies(row_of(k)):
            copy.start()
        return carry

    lax.fori_loop(0, 5, start_row, 0)
    lax.fori_loop(0, 1, start_rest, 0)

    pl.semaphore_wait(barrier, bits + has_low.astype(jnp.int32) + has_high.astype(jnp.int32))

    @pl.when(has_low)
    def _():
        for copy in halo_copies(False):
            copy.start()

    @pl.when(has_high)
    def _():
        for copy in halo_copies(True):
            copy.start()

    lax.fori_loop(5, height, start_row, 0)
    lax.fori_loop(1, height, start_rest, 0)

    moment[...] = jnp.zeros_like(moment)
    anom_b[...] = jnp.zeros_like(anom_b)
    here = lax.broadcasted_iota(jnp.int32, (lons, lons), 0)
    there = lax.broadcasted_iota(jnp.int32, (lons, lons), 1)
    ahead = there - here
    right = (ahead == 1) | (ahead == 1 - lons)
    left = (ahead == -1) | (ahead == lons - 1)
    shift[...] = jnp.where(right, 6.0, jnp.where(left, -6.0, 0.0)).astype(BF16)

    def factors(r, carry):
        def spread(ref):
            return jnp.broadcast_to(ref[pl.ds(r, 1), :], (levels, lons)).T

        f[r] = spread(scale_ref) * (1.0 / 12.0)
        c[r] = spread(balance_ref) * heat_slope_ref[...]
        return carry

    lax.fori_loop(0, height, factors, 0)

    @pl.when(jnp.logical_not(has_low))
    def _():
        u[:, pl.ds(0, 2)] = jnp.zeros((members, 2, lons, levels), BF16)
        v[:, pl.ds(0, 2)] = jnp.zeros((members, 2, lons, levels), BF16)

    @pl.when(jnp.logical_not(has_high))
    def _():
        u[:, pl.ds(height + 2, 2)] = jnp.zeros((members, 2, lons, levels), BF16)
        v[:, pl.ds(height + 2, 2)] = jnp.zeros((members, 2, lons, levels), BF16)

    def receive_low():
        for copy in halo_copies(True):
            copy.wait_recv()

    def receive_high():
        for copy in halo_copies(False):
            copy.wait_recv()

    def wait_row(r, carry):
        for copy in wind_copies(r):
            copy.wait()
        return carry

    lax.fori_loop(0, 4, wait_row, 0)

    def gram(a, times):
        cut = a.shape[1] // 2
        top = lax.dot_general(
            a[:, :cut], a, (((0,), (0,)), ((), ())), preferred_element_type=F32
        )
        low = lax.dot_general(
            a[:, cut:], a[:, cut:], (((0,), (0,)), ((), ())), preferred_element_type=F32
        )
        moment[:cut, :] += top if times == 1 else times * top
        moment[cut:, cut:] += low if times == 1 else times * low

    def longitude(dlon, e, side):
        at = slice(side * half, (side + 1) * half)
        for m in range(members):
            both = jnp.concatenate([v[m, e], u[m, e]], axis=1)
            dlon[m] = jnp.dot(shift[at, :], both, preferred_element_type=F32)

    def merge(t, k):
        for stream in range(2):
            mean_copy(t, stream, k).wait_recv()
            first = starts[t] + stream * sizes[t]
            at = slice(first, first + sizes[t])
            mine = piece(t, stream, k, True)[...].astype(F32)
            theirs = got[k, at].astype(F32)
            away[k, at] = ((mine - theirs) * 2.0 ** (t / 2)).astype(BF16)
            if t + 1 < bits:
                kept[k, at] = (0.5 * (mine + theirs)).astype(BF16)
                mean_copy(t + 1, stream, k).start()
        if t + 1 == bits:
            gram(away[k], 0.5 * members)

    def row(k, carry):
        r = row_of(k)
        e = r + 2
        inner = height - 4

        @pl.when(k < inner)
        def _():
            wait_row(k + 4, 0)

        @pl.when((k == inner) & even & has_high | (k == inner + 2) & jnp.logical_not(even) & has_high)
        def _():
            receive_high()

        @pl.when((k == inner + 2) & even & has_low | (k == inner) & jnp.logical_not(even) & has_low)
        def _():
            receive_low()

        for copy in rest_copies(r):
            copy.wait()
        def chunk(side, dlon, anom, i, carry):
            within = pl.ds(pl.multiple_of(i * CHUNK, CHUNK), CHUNK)
            at = pl.ds(pl.multiple_of(side * half + i * CHUNK, CHUNK), CHUNK)
            factor = f[r, at, :]
            curl_factor = c[r, at, :]
            slope = slope_ref[...]
            held, total = [], None
            for m in range(members):

                def wind(ref, d):
                    return ref[m, e + d, at, :].astype(F32)

                def lat(ref):
                    return 8.0 * (wind(ref, 1) - wind(ref, -1)) - (wind(ref, 2) - wind(ref, -2))

                curl = factor * (dlon[m, within, :levels] - lat(u))
                spread = factor * (dlon[m, within, levels:] + lat(v))
                heat = h[m, r, at, :].astype(F32) - curl_factor * curl
                moist = q[m, r, at, :].astype(F32) - slope * heat
                state = (curl, spread, heat, moist)
                held.append(state)
                total = state if total is None else tuple(a + b for a, b in zip(total, state))
            mean = tuple(a * (1.0 / members) for a in total)
            for n in range(4):
                lanes = slice(n * levels, (n + 1) * levels)
                mean_rows[k, at, lanes] = mean[n].astype(BF16)
                for m in range(members):
                    to = pl.ds(pl.multiple_of(m * half + i * CHUNK, CHUNK), CHUNK)
                    anom[to, lanes] = (held[m][n] - mean[n]).astype(BF16)
            return carry

        steps = half // CHUNK
        gram(anom_b[...], 1)
        longitude(dlon_b, e, 1)
        lax.fori_loop(0, steps, functools.partial(chunk, 0, dlon_a, anom_a), 0, unroll=True)
        gram(anom_a[...], 1)
        longitude(dlon_a, row_of(jnp.minimum(k + 1, height - 1)) + 2, 0)
        lax.fori_loop(0, steps, functools.partial(chunk, 1, dlon_b, anom_b), 0, unroll=True)
        for stream in range(2):
            mean_copy(0, stream, k).start()
        for t in range(bits):

            @pl.when(k > t)
            def _():
                merge(t, k - t - 1)

        return carry

    longitude(dlon_a, row_of(0) + 2, 0)
    lax.fori_loop(0, height, row, 0)
    gram(anom_b[...], 1)
    for k in range(height, height + bits):
        for t in range(bits):
            if k - t - 1 < height:
                merge(t, k - t - 1)
    cut = moment.shape[0] // 2
    moment[cut:, :cut] = moment[:cut, cut:].T
    for flip in flips(0):
        for stream in range(2):
            part_copy(0, stream, flip).start()
    for t in range(bits):
        if t + 1 < bits:
            for stream in range(2):
                for flip in flips(t):
                    if flip[0]:
                        take(t, stream, flip)
                for flip in flips(t + 1):
                    part_copy(t + 1, stream, flip).start()
        for stream in range(2):
            for flip in flips(t):
                if t + 1 == bits or not flip[0]:
                    take(t, stream, flip)
    out_ref[...] = moment[pl.ds(pl.multiple_of(me * block, block), block), :]

    def sent(k, carry):
        for t in range(bits):
            for stream in range(2):
                mean_copy(t, stream, k).wait_send()
        return carry

    lax.fori_loop(0, height, sent, 0)
    for t in range(bits):
        for stream in range(2):
            for flip in flips(t):
                part_copy(t, stream, flip).wait_send()

    @pl.when(has_low)
    def _():
        for copy in halo_copies(False):
            copy.wait_send()

    @pl.when(has_high)
    def _():
        for copy in halo_copies(True):
            copy.wait_send()


def on_device(u, v, h, q, projection_scale, balance_multiplier, heat_slope, moist_slope):
    members, height, lons, levels = u.shape
    groups = lax.axis_size("member")
    bands = lax.axis_size("space")
    width = 4 * levels
    scale = 1.0 / ((members * groups - 1) * height * lons)
    shape = (height, lons, levels)
    block, others = width // groups, groups - 1
    bits = groups.bit_length() - 1
    merged = lons - lons // groups
    hbm = pl.BlockSpec(memory_space=pl.ANY)
    vmem = pl.BlockSpec(memory_space=pltpu.VMEM)
    dma = pltpu.SemaphoreType.DMA

    def body(*refs):
        kernel(groups, bands, *refs)

    out = pl.pallas_call(
        body,
        out_shape=jax.ShapeDtypeStruct((block, width), F32),
        in_specs=[hbm] * 4 + [vmem] * 4,
        out_specs=vmem,
        scratch_shapes=[
            pltpu.VMEM((members, height + 4, lons, levels), BF16),
            pltpu.VMEM((members, height + 4, lons, levels), BF16),
            pltpu.VMEM((members, height, lons, levels), BF16),
            pltpu.VMEM((members, height, lons, levels), BF16),
            pltpu.VMEM(shape, F32),
            pltpu.VMEM(shape, F32),
            pltpu.VMEM((lons, lons), BF16),
            pltpu.VMEM((members, lons // 2, 2 * levels), F32),
            pltpu.VMEM((members, lons // 2, 2 * levels), F32),
            pltpu.VMEM((members * lons // 2, width), BF16),
            pltpu.VMEM((members * lons // 2, width), BF16),
            pltpu.VMEM((height, lons, width), BF16),
            pltpu.VMEM((height, merged, width), BF16),
            pltpu.VMEM((height, merged, width), BF16),
            pltpu.VMEM((height, merged, width), BF16),
            pltpu.VMEM((width, width), F32),
            pltpu.VMEM((2, others, block, width // 2), F32),
            dma((height, 2)),
            dma((height, 2)),
            dma((2, 2)),
            dma((2, 2)),
            dma((height, bits, 2)),
            dma((height, bits, 2)),
            dma((2, others)),
            dma((2, others)),
        ],
        compiler_params=pltpu.CompilerParams(
            collective_id=0, has_side_effects=True, vmem_limit_bytes=56 * 2**20
        ),
        cost_estimate=pl.CostEstimate(
            flops=2 * members * height * lons * width * width,
            bytes_accessed=16 * 2**20,
            transcendentals=0,
        ),
        name="band_moments",
    )(u, v, h, q, projection_scale, balance_multiplier, heat_slope[None], moist_slope[None])
    return (out * scale)[None]


def solution(mesh):
    placed = (
        P("member", "space", None, None),
        P("member", "space", None, None),
        P("member", "space", None, None),
        P("member", "space", None, None),
        P("space", None),
        P("space", None),
        P(),
        P(),
    )
    return jax.shard_map(
        on_device, mesh=mesh, in_specs=placed, out_specs=P("space", "member", None), check_vma=False
    )
```
